32 devices in a mesh: fsdp: 4 (over z), ctx: 4 (over x, core), tp: 2 (over y).
Axes of the slice: x: 2, y: 2, z: 4, core: 2. Of those that a mesh axis runs over, the one named last changes fastest.
Arguments:
- hidden_in: bfloat16 [4, 1024, 1024], P('fsdp', 'ctx'), may hold values from -6 to 6
- piece_starts: int32 [4, 2], P('fsdp'), may hold values from 0 to 768, as said below
- ln1_gain: bfloat16 [2, 1024], P(None, 'fsdp'), may hold values from 0.5 to 1.5
- ln1_shift: bfloat16 [2, 1024], P(None, 'fsdp'), may hold values from -3 to 3
- qkv_weight: bfloat16 [2, 1024, 3, 1024], P(None, 'fsdp', None, 'tp'), may hold values from -0.1875 to 0.1875
- qv_bias: bfloat16 [2, 2, 8, 128], P(None, None, 'tp', 'fsdp'), may hold values from -4 to 4
- dense_weight: bfloat16 [2, 1024, 1024], P(None, 'tp', 'fsdp'), may hold values from -0.75 to 0.75
- dense_bias: bfloat16 [2, 1024], P(None, 'fsdp'), may hold values from -3 to 3
- ln2_gain: bfloat16 [2, 1024], P(None, 'fsdp'), may hold values from 0.5 to 1.5
- ln2_shift: bfloat16 [2, 1024], P(None, 'fsdp'), may hold values from -3 to 3
- up_weight: bfloat16 [2, 1024, 4096], P(None, 'fsdp', 'tp'), may hold values from -0.1875 to 0.1875
- up_bias: bfloat16 [2, 32, 128], P(None, 'tp', 'fsdp'), may hold values from -4 to 4
- down_weight: bfloat16 [2, 4096, 1024], P(None, 'tp', 'fsdp'), may hold values from -0.09375 to 0.09375
- down_bias: bfloat16 [2, 1024], P(None, 'fsdp'), may hold values from -3 to 3
- out_grad: bfloat16 [4, 1024, 1024], P('fsdp', 'ctx'), may hold values from -6 to 6
Outputs:
- hidden_out: bfloat16 [4, 1024, 1024], P('fsdp', 'ctx')
- input_grad: float32 [4, 1024, 1024], P('fsdp', 'ctx')
- ln1_gain_grad: float32 [2, 1024], P(None, 'fsdp')
- ln1_shift_grad: float32 [2, 1024], P(None, 'fsdp')
- qkv_weight_grad: float32 [2, 1024, 3, 1024], P(None, 'fsdp', None, 'tp')
- qv_bias_grad: float32 [2, 2, 8, 128], P(None, None, 'tp', 'fsdp')
- dense_weight_grad: float32 [2, 1024, 1024], P(None, 'tp', 'fsdp')
- dense_bias_grad: float32 [2, 1024], P(None, 'fsdp')
- ln2_gain_grad: float32 [2, 1024], P(None, 'fsdp')
- ln2_shift_grad: float32 [2, 1024], P(None, 'fsdp')
- up_weight_grad: float32 [2, 1024, 4096], P(None, 'fsdp', 'tp')
- up_bias_grad: float32 [2, 32, 128], P(None, 'tp', 'fsdp')
- down_weight_grad: float32 [2, 4096, 1024], P(None, 'tp', 'fsdp')
- down_bias_grad: float32 [2, 1024], P(None, 'fsdp')
The draws below stay inside these ranges and needn't reach their ends.
Inputs may be any that keep to these rules, and one draw needn't show every extreme that they name: `piece_starts`: each sequence holds 2 disjoint pieces of 256 positions, in rising order, each inside the sequence.
All inputs are finite; a program needn't handle non-finite values.
Results may differ from the reference program's by a relative error of at most 0.014.
Values may be sent and summed in bfloat16 or wider, within the bound.
No kernel may reach another device: no remote copies, remote signals or barrier semaphores. Data moves between devices by JAX's collectives and lax.ppermute only.
A program may use at most 192 MiB of HBM per device.

```python
import math
import jax
import jax.numpy as jnp
from jax import lax

D = 1024
HEADS = 16
FF = 4096
HEAD = 64
LAYERS = 2
PIECE = 256
PIECES = 2
LEN = 1024
SEQS = 4


def draw_piece_starts(key, part):
    slot_width = LEN // PIECES
    offsets = jax.random.randint(jax.random.fold_in(key, 11), (SEQS, PIECES), 0, slot_width - PIECE + 1)
    starts = jnp.arange(PIECES, dtype=jnp.int32)[None, :] * slot_width + offsets
    late_row = jax.random.randint(jax.random.fold_in(key, 12), (), 0, SEQS)
    early_row = jax.random.randint(jax.random.fold_in(key, 13), (), 0, SEQS)
    row_index = jnp.arange(SEQS, dtype=jnp.int32)[:, None]
    col_index = jnp.arange(PIECES, dtype=jnp.int32)[None, :]
    starts = jnp.where((row_index == late_row) & (col_index == PIECES - 1), LEN - PIECE, starts)
    starts = jnp.where((row_index == early_row) & (col_index == 0), 0, starts)
    return starts.astype(jnp.int32)


def levels(stream_key, shape, shards, low, high):
    def one(axis_at, shards_of):
        steps = jax.random.uniform(jax.random.fold_in(jax.random.fold_in(stream_key, 6), axis_at), (shards_of,), jnp.float32, low / len(shards), high / len(shards))
        return jnp.repeat(jnp.exp(steps), shape[axis_at] // shards_of).reshape((-1,) + (1,) * (len(shape) - axis_at - 1))

    factor_of = one(*shards[0])
    for cut in shards[1:]:
        factor_of = factor_of * one(*cut)
    return factor_of


def scatter_about(stream_key, shape, scale, limit, split=(), kind=jnp.bfloat16):
    level = levels(stream_key, shape, split, -0.22, 0.18) if split else 1.0
    values = jax.random.normal(stream_key, shape, jnp.float32) * scale * level
    return jnp.minimum(jnp.maximum(values, -limit), limit).astype(kind)


def setup_inputs(seed: int = 0) -> dict:
    key_of = jax.random.split(jax.random.key(seed), 16)
    return {
        "hidden_in": scatter_about(key_of[0], (SEQS, LEN, D), 1.0, 6.0, ((0, 4), (1, 4))),
        "piece_starts": draw_piece_starts(jax.random.fold_in(key_of[15], 71), 0),
        "ln1_gain": jnp.clip(1.0 + 0.1 * jax.random.normal(key_of[2], (LAYERS, D), jnp.float32), 0.5, 1.5).astype(jnp.bfloat16),
        "ln1_shift": scatter_about(key_of[3], (LAYERS, D), 0.3, 3.0, ((1, 4),)),
        "qkv_weight": scatter_about(key_of[4], (LAYERS, D, 3, D), D ** -0.5, 0.1875, ((1, 4), (3, 2))),
        "qv_bias": scatter_about(key_of[5], (LAYERS, 2, D // 128, 128), 0.5, 4.0, ((2, 2), (3, 4))),
        "dense_weight": scatter_about(key_of[6], (LAYERS, D, D), (D // 16) ** -0.5, 0.75, ((1, 2), (2, 4))),
        "dense_bias": scatter_about(key_of[7], (LAYERS, D), 0.3, 3.0, ((1, 4),)),
        "ln2_gain": jnp.clip(1.0 + 0.1 * jax.random.normal(key_of[8], (LAYERS, D), jnp.float32), 0.5, 1.5).astype(jnp.bfloat16),
        "ln2_shift": scatter_about(key_of[9], (LAYERS, D), 0.3, 3.0, ((1, 4),)),
        "up_weight": scatter_about(key_of[10], (LAYERS, D, FF), D ** -0.5, 0.1875, ((1, 4), (2, 2))),
        "up_bias": scatter_about(key_of[11], (LAYERS, FF // 128, 128), 0.5, 4.0, ((1, 2), (2, 4))),
        "down_weight": scatter_about(key_of[12], (LAYERS, FF, D), FF ** -0.5, 0.09375, ((1, 2), (2, 4))),
        "down_bias": scatter_about(key_of[13], (LAYERS, D), 0.3, 3.0, ((1, 4),)),
        "out_grad": scatter_about(key_of[14], (SEQS, LEN, D), 1.0, 6.0, ((0, 4), (1, 4))),
    }


MATMUL_ACCURACY = lax.Precision.HIGHEST

@jax.custom_vjp
def low(v):
    return lax.optimization_barrier(v.astype(jnp.bfloat16)).astype(jnp.float32)

@jax.custom_vjp
def lowered_backward(v):
    return v

def low_keep(v):
    return (low(v), None)

def low_pass(kept, grad):
    return (grad,)

def back_keep(v):
    return (v, None)

def back_low(kept, grad):
    return (low(grad),)
low.defvjp(low_keep, low_pass)
lowered_backward.defvjp(back_keep, back_low)

def both_ways(v):
    return lowered_backward(low(v))

def normalize(v, norm_gain, norm_shift):
    row_mean = lax.optimization_barrier(jnp.mean(v, axis=-1, keepdims=True))
    centred = v - row_mean
    variance = lax.optimization_barrier(jnp.mean(centred * centred, axis=-1, keepdims=True))
    return centred * lax.rsqrt(variance + 1e-05) * norm_gain + norm_shift

def piece_labels(starts, positions):
    inside = (positions >= starts[..., :, None]) & (positions < starts[..., :, None] + PIECE)
    labels = jnp.arange(1, starts.shape[-1] + 1, dtype=jnp.int32)
    return lax.optimization_barrier(jnp.sum(jnp.where(inside, labels[:, None], 0), axis=-2)).astype(jnp.int32)

def head_attention(element):
    query_head, key_head, value_head, head_slope, own_starts = element
    length = query_head.shape[0]
    positions = jnp.arange(length, dtype=jnp.int32)
    labels = piece_labels(own_starts, positions)
    visible = (positions[None, :] <= positions[:, None]) | (labels[:, None] > 0) & (labels[:, None] == labels[None, :])
    distance = jnp.abs(positions[:, None] - positions[None, :]).astype(jnp.float32)
    raw_scores = jnp.einsum('qe,ke->qk', query_head, key_head, precision=MATMUL_ACCURACY) * (1.0 / math.sqrt(HEAD)) - head_slope * distance
    scores = lowered_backward(jnp.where(visible, raw_scores, -1e+30))
    row_max = lax.optimization_barrier(jnp.max(scores, axis=-1, keepdims=True))
    exponent = jnp.exp(scores - row_max)
    probability = low(exponent / lax.optimization_barrier(jnp.sum(exponent, axis=-1, keepdims=True)))
    return jnp.einsum('qk,ke->qe', probability, value_head, precision=MATMUL_ACCURACY)

def attention(queries, key_rows, value_rows, starts):
    seq_count, length = (queries.shape[0], queries.shape[1])

    def heads_first(t):
        return jnp.transpose(t.reshape(seq_count, length, HEADS, HEAD), (0, 2, 1, 3)).reshape(seq_count * HEADS, length, HEAD)
    slopes = jnp.exp2(-(jnp.arange(HEADS).astype(jnp.float32) + 1.0) * 0.5) * (4.0 / length)
    element_list = (heads_first(queries), heads_first(key_rows), heads_first(value_rows), jnp.tile(slopes, seq_count), jnp.repeat(starts, HEADS, axis=0))
    outputs = lax.map(jax.checkpoint(head_attention), element_list)
    return jnp.transpose(outputs.reshape(seq_count, HEADS, length, HEAD), (0, 2, 1, 3)).reshape(seq_count, length, HEADS * HEAD)

def apply_layer(x, weights, starts):
    gain_one, shift_one, query_key_value_weight, b_qv, dense_out_weight, dense_out_bias, gain_two, shift_two, up_proj_weight, up_proj_bias, down_proj_weight, down_proj_bias = weights
    normed_input = low(normalize(x, gain_one, shift_one))
    query_key_value = jnp.einsum('qhm,mvy->qhvy', normed_input, query_key_value_weight, precision=MATMUL_ACCURACY)
    bias_rows = b_qv.reshape(2, -1)
    queries = both_ways(query_key_value[:, :, 0] + bias_rows[0])
    key_rows = both_ways(query_key_value[:, :, 1])
    value_rows = both_ways(query_key_value[:, :, 2] + bias_rows[1])
    attended_output = both_ways(attention(queries, key_rows, value_rows, starts))
    branch_output = lowered_backward(jnp.einsum('nkr,rh->nkh', attended_output, dense_out_weight, precision=MATMUL_ACCURACY) + dense_out_bias)
    middle = x + branch_output
    second_normed = low(normalize(middle, gain_two, shift_two))
    inner_activation = lowered_backward(jnp.einsum('rbk,kx->rbx', second_normed, up_proj_weight, precision=MATMUL_ACCURACY) + up_proj_bias.reshape(-1))
    active_units = low(jax.nn.gelu(inner_activation, approximate=True))
    second_branch = lowered_backward(jnp.einsum('zxk,kh->zxh', active_units, down_proj_weight, precision=MATMUL_ACCURACY) + down_proj_bias)
    return middle + second_branch

def reference(hidden_in, piece_starts, ln1_gain, ln1_shift, qkv_weight, qv_bias, dense_weight, dense_bias, ln2_gain, ln2_shift, up_weight, up_bias, down_weight, down_bias, out_grad):
    weights = tuple((w.astype(jnp.float32) for w in (ln1_gain, ln1_shift, qkv_weight, qv_bias, dense_weight, dense_bias, ln2_gain, ln2_shift, up_weight, up_bias, down_weight, down_bias)))

    def forward(x, *params):
        for layer_index in range(LAYERS):
            x = apply_layer(x, tuple((p[layer_index] for p in params)), piece_starts)
        return x
    result, pullback = jax.vjp(forward, hidden_in.astype(jnp.float32), *weights)
    gradients = pullback(out_grad.astype(jnp.float32))
    return (result.astype(jnp.bfloat16), gradients[0], gradients[1], gradients[2], gradients[3], gradients[4], gradients[5], gradients[6], gradients[7], gradients[8], gradients[9], gradients[10], gradients[11], gradients[12])
```

```python
import functools
import math

import jax
import jax.numpy as jnp
from jax import lax
from jax.experimental import pallas as pl
from jax.experimental.pallas import tpu as pltpu
from jax.sharding import PartitionSpec as P

HEAD = 64
PIECE = 256
FAR = 1e30
BF = jnp.bfloat16
F32 = jnp.float32
INV_ROOT = 1.0 / math.sqrt(HEAD)
NT = (((1,), (1,)), ((), ()))
TN = (((0,), (0,)), ((), ()))
NN = (((1,), (0,)), ((), ()))


def mm(a, b, dims):
    return lax.dot_general(a, b, dims, preferred_element_type=F32)


def reach(q_meta_ref, k_meta_ref):
    delta = q_meta_ref[0:1, :] - k_meta_ref[:, 0:1]
    seen = (delta >= 0.0) | (q_meta_ref[1:2, :] == k_meta_ref[:, 1:2])
    return jnp.where(seen, jnp.abs(delta), FAR)


def lanes_of(width, head):
    lane = lax.broadcasted_iota(jnp.int32, (1, width), 1)
    return (lane // HEAD) == head


def forward_kernel(slope_ref, q_meta_ref, k_meta_ref, q_ref, k_ref, v_ref, o_ref, lse_ref, *, width):
    dist = reach(q_meta_ref, k_meta_ref)
    pairs = q_ref.shape[1] // width
    per = width // HEAD
    for pair in range(pairs):
        at = slice(pair * width, (pair + 1) * width)
        q = q_ref[:, at] * jnp.asarray(INV_ROOT, BF)
        k = k_ref[:, at]
        v = v_ref[:, at]
        outs = []
        for head in range(per):
            index = pair * per + head
            q_head = q if per == 1 else jnp.where(lanes_of(width, head), q, jnp.zeros_like(q))
            s = mm(k, q_head, NT) - slope_ref[index] * dist
            top = jnp.max(s, axis=0, keepdims=True)
            e = jnp.exp(s - top)
            z = jnp.sum(e, axis=0, keepdims=True)
            lse_ref[index : index + 1, :] = top + jnp.log(z)
            outs.append(mm(v, e.astype(BF), TN) / z)
        if per == 1:
            out = outs[0]
        else:
            row = lax.broadcasted_iota(jnp.int32, (width, 1), 0)
            out = jnp.where(row < HEAD, outs[0], outs[1])
        o_ref[:, at] = out.T.astype(BF)


def backward_kernel(
    slope_ref, q_meta_ref, k_meta_ref, q_ref, k_ref, v_ref, do_ref, lse_ref, dq_ref, dk_ref, dv_ref, dk_acc, dv_acc, *, width
):
    step = pl.program_id(0)

    @pl.when(step == 0)
    def _():
        dk_acc[...] = jnp.zeros_like(dk_acc)
        dv_acc[...] = jnp.zeros_like(dv_acc)

    dist = reach(q_meta_ref, k_meta_ref)
    pairs = q_ref.shape[1] // width
    per = width // HEAD
    for pair in range(pairs):
        at = slice(pair * width, (pair + 1) * width)
        q = q_ref[:, at] * jnp.asarray(INV_ROOT, BF)
        k = k_ref[:, at]
        v = v_ref[:, at]
        do = do_ref[:, at]
        dqs = []
        for head in range(per):
            index = pair * per + head
            mine = None if per == 1 else lanes_of(width, head)
            q_head = q if per == 1 else jnp.where(mine, q, jnp.zeros_like(q))
            do_head = do if per == 1 else jnp.where(mine, do, jnp.zeros_like(do))
            s = mm(k, q_head, NT) - slope_ref[index] * dist
            p = jnp.exp(s - lse_ref[index : index + 1, :])
            dp = mm(v, do_head, NT)
            inner = jnp.sum(p * dp, axis=0, keepdims=True)
            ds = (p * (dp - inner)).astype(BF)
            dqs.append(mm(k, ds, TN))
            dk_acc[:, at] += mm(ds, q_head, NN)
            dv_acc[:, at] += mm(p.astype(BF), do_head, NN)
        if per == 1:
            dq = dqs[0]
        else:
            row = lax.broadcasted_iota(jnp.int32, (width, 1), 0)
            dq = jnp.where(row < HEAD, dqs[0], dqs[1])
        dq_ref[:, at] = (dq.T * INV_ROOT).astype(BF)

    @pl.when(step == pl.num_programs(0) - 1)
    def _():
        dk_ref[...] = dk_acc[...].astype(BF)
        dv_ref[...] = dv_acc[...].astype(BF)


def attention_setup(q, k):
    tokens, columns = q.shape
    keys = k.shape[0]
    width = min(128, columns)
    block = min(tokens, 256 if keys <= 1024 else 128)
    heads = columns // HEAD
    whole = lambda shape: pl.BlockSpec(shape, lambda i: (0,) * len(shape))
    specs = [
        pl.BlockSpec(memory_space=pltpu.SMEM),
        pl.BlockSpec((8, block), lambda i: (0, i)),
        whole((keys, 128)),
        pl.BlockSpec((block, columns), lambda i: (i, 0)),
        whole((keys, columns)),
        whole((keys, columns)),
    ]
    return tokens, columns, keys, width, block, heads, whole, specs


def attend_forward(slopes, q_meta, k_meta, q, k, v):
    tokens, columns, keys, width, block, heads, whole, specs = attention_setup(q, k)
    return pl.pallas_call(
        functools.partial(forward_kernel, width=width),
        grid=(tokens // block,),
        in_specs=specs,
        out_specs=[
            pl.BlockSpec((block, columns), lambda i: (i, 0)),
            pl.BlockSpec((heads, block), lambda i: (0, i)),
        ],
        out_shape=[
            jax.ShapeDtypeStruct((tokens, columns), BF),
            jax.ShapeDtypeStruct((heads, tokens), F32),
        ],
        compiler_params=pltpu.CompilerParams(vmem_limit_bytes=40 * 2**20),
        cost_estimate=pl.CostEstimate(
            flops=4 * tokens * keys * columns * 4, bytes_accessed=4 * keys * columns * 2, transcendentals=heads * tokens * keys
        ),
        name="attend_forward",
    )(slopes, q_meta, k_meta, q, k, v)


def attend_backward(slopes, q_meta, k_meta, q, k, v, do, lse):
    tokens, columns, keys, width, block, heads, whole, specs = attention_setup(q, k)
    return pl.pallas_call(
        functools.partial(backward_kernel, width=width),
        grid=(tokens // block,),
        in_specs=specs
        + [
            pl.BlockSpec((block, columns), lambda i: (i, 0)),
            pl.BlockSpec((heads, block), lambda i: (0, i)),
        ],
        out_specs=[
            pl.BlockSpec((block, columns), lambda i: (i, 0)),
            whole((keys, columns)),
            whole((keys, columns)),
        ],
        out_shape=[
            jax.ShapeDtypeStruct((tokens, columns), BF),
            jax.ShapeDtypeStruct((keys, columns), BF),
            jax.ShapeDtypeStruct((keys, columns), BF),
        ],
        scratch_shapes=[pltpu.VMEM((keys, columns), F32), pltpu.VMEM((keys, columns), F32)],
        compiler_params=pltpu.CompilerParams(vmem_limit_bytes=40 * 2**20),
        cost_estimate=pl.CostEstimate(
            flops=10 * tokens * keys * columns * 4, bytes_accessed=8 * keys * columns * 2, transcendentals=heads * tokens * keys
        ),
        name="attend_backward",
    )(slopes, q_meta, k_meta, q, k, v, do, lse)


def statistics(v):
    mean = jnp.mean(v, axis=-1, keepdims=True)
    centred = v - mean
    variance = jnp.mean(centred * centred, axis=-1, keepdims=True)
    scale = lax.rsqrt(variance + 1e-05)
    return centred * scale, scale


def normalize(v, gain, shift):
    return statistics(v)[0] * gain + shift


def normalize_back(v, gain, grad):
    hat, scale = statistics(v)
    pulled = grad * gain
    first = jnp.mean(pulled, axis=-1, keepdims=True)
    second = jnp.mean(pulled * hat, axis=-1, keepdims=True)
    return scale * (pulled - first - hat * second), jnp.sum(grad * hat, axis=0), jnp.sum(grad, axis=0)


C0 = math.sqrt(2.0 / math.pi)
C1 = 0.044715


def gelu_tanh(t):
    return 0.5 * t * (1.0 + jnp.tanh(C0 * (t + C1 * t * t * t)))


def gelu_slope(t):
    bent = jnp.tanh(C0 * (t + C1 * t * t * t))
    return 0.5 * (1.0 + bent) + 0.5 * t * (1.0 - bent * bent) * (C0 * (1.0 + 3.0 * C1 * t * t))


def local(
    fsdp,
    outer,
    tp,
    hidden_in,
    piece_starts,
    ln1_gain,
    ln1_shift,
    qkv_weight,
    qv_bias,
    dense_weight,
    dense_bias,
    ln2_gain,
    ln2_shift,
    up_weight,
    up_bias,
    down_weight,
    down_bias,
    out_grad,
):
    layers, rows_f, _, half = qkv_weight.shape
    group_len, d = hidden_in.shape[1:]
    hidden_half = up_weight.shape[2]
    quarter = half // outer
    own = quarter // 2
    hidden_quarter = hidden_half // outer
    hidden_own = hidden_quarter // 2
    rows = group_len // tp
    length = group_len * 2 * outer

    f = lax.axis_index("fsdp")
    ctx = lax.axis_index("ctx")
    t = lax.axis_index("tp")
    x, c = ctx // 2, ctx % 2

    def fetch(v, dx, dc, dt):
        pairs = []
        for xi in range(outer):
            for ci in range(2):
                for ti in range(tp):
                    src = (((xi + dx) % outer) * 2 + (ci + dc) % 2) * tp + (ti + dt) % tp
                    pairs.append((src, (xi * 2 + ci) * tp + ti))
        return lax.ppermute(v, ("ctx", "tp"), pairs)

    def fetch_f(v, df):
        return lax.ppermute(v, "fsdp", [((i + df) % fsdp, i) for i in range(fsdp)])

    slots = [(dx, dt) for dx in range(outer) for dt in range(tp)]

    def gather(v):
        return jnp.concatenate([v] + [fetch(v, dx, 0, dt) for dx, dt in slots[1:]], axis=0)

    def scatter(v):
        parts = [v[i * rows : (i + 1) * rows] for i in range(len(slots))]
        total = parts[0]
        for part, (dx, dt) in zip(parts[1:], slots[1:]):
            total = total + fetch(part.astype(BF), -dx, 0, -dt).astype(F32)
        return total

    def spread_input(v):
        out = []
        for dx in range(outer):
            block = v if dx == 0 else fetch(v, dx, 0, 0)
            for dt in range(tp):
                out.append(lax.dynamic_slice_in_dim(block, ((t + dt) % tp) * rows, rows, 0))
        return jnp.concatenate(out, axis=0)

    small = jnp.concatenate(
        [v.reshape(-1) for v in (ln1_gain, ln1_shift, dense_bias, ln2_gain, ln2_shift, down_bias, qv_bias, up_bias)]
    )
    count = small.shape[0]
    padded = -(-count // 2048) * 2048
    small = jnp.pad(small, (0, padded - count)).reshape(-1, 128)
    held = jnp.stack([small] + [fetch_f(small, k) for k in range(1, fsdp)])
    smalls = jnp.concatenate([lax.dynamic_index_in_dim(held, (j - f) % fsdp, 0) for j in range(fsdp)], axis=0)
    smalls = smalls.reshape(fsdp, -1).astype(F32)
    place = 0
    vectors = []
    for _ in range(6):
        piece = smalls[:, place : place + layers * rows_f].reshape(fsdp, layers, rows_f)
        vectors.append(jnp.transpose(piece, (1, 0, 2)).reshape(layers, d))
        place += layers * rows_f
    gain_one, shift_one, bias_dense, gain_two, shift_two, bias_down = vectors
    blocks_qv, lane_f = qv_bias.shape[2:]
    piece = smalls[:, place : place + layers * 2 * blocks_qv * lane_f].reshape(fsdp, layers, 2, blocks_qv, lane_f)
    bias_qv = jnp.transpose(piece, (1, 2, 3, 0, 4)).reshape(layers, 2, half)
    place += layers * 2 * blocks_qv * lane_f
    blocks_up = up_bias.shape[1]
    piece = smalls[:, place : place + layers * blocks_up * lane_f].reshape(fsdp, layers, blocks_up, lane_f)
    bias_up = jnp.transpose(piece, (1, 2, 0, 3)).reshape(layers, hidden_half)

    def own_first(v, width):
        mine = lax.dynamic_slice_in_dim(v, (x * 2 + c) * width, width, v.ndim - 1)
        others = lax.dynamic_slice_in_dim(v, (x * 2 + 1 - c) * width, width, v.ndim - 1)
        return jnp.concatenate([mine, others], axis=-1)

    bias_qv = own_first(bias_qv, own)
    bias_up = own_first(bias_up, hidden_own)

    at = (x * 2 + c) * own
    at_hidden = (x * 2 + c) * hidden_own
    attention_own, feed_own = [], []
    for layer in range(layers):
        qkv = lax.dynamic_slice_in_dim(qkv_weight[layer], at, own, 2).reshape(rows_f, 3 * own)
        dense = lax.dynamic_slice_in_dim(dense_weight[layer], at, own, 0).T
        attention_own.append(lax.all_gather(jnp.concatenate([qkv, dense], axis=1), "fsdp", axis=0, tiled=True))
        up = lax.dynamic_slice_in_dim(up_weight[layer], at_hidden, hidden_own, 1)
        down = lax.dynamic_slice_in_dim(down_weight[layer], at_hidden, hidden_own, 0).T
        feed_own.append(lax.all_gather(jnp.concatenate([up, down], axis=1), "fsdp", axis=0, tiled=True))
    attention_both = [(w, fetch(w, 0, 1, 0)) for w in attention_own]
    feed_both = [(w, fetch(w, 0, 1, 0)) for w in feed_own]

    row_ids = jnp.arange(rows, dtype=jnp.int32)

    def positions_of(core):
        return jnp.concatenate(
            [
                (((x + dx) % outer) * 2 + core) * group_len + ((t + dt) % tp) * rows + row_ids
                for dx, dt in slots
            ]
        )

    def labels_of(positions):
        starts = piece_starts[0]
        inside = (positions[None, :] >= starts[:, None]) & (positions[None, :] < starts[:, None] + PIECE)
        ids = jnp.arange(1, starts.shape[0] + 1, dtype=jnp.int32)
        return jnp.sum(jnp.where(inside, ids[:, None], 0), axis=0)

    here, there = positions_of(c), positions_of(1 - c)
    keys_at = jnp.concatenate([here, there])
    q_label = labels_of(here)
    k_label = labels_of(keys_at)
    q_meta = jnp.stack([here, jnp.where(q_label > 0, q_label, -1)]).astype(F32)
    q_meta = jnp.pad(q_meta, ((0, 6), (0, 0)))
    k_meta = jnp.stack([keys_at, jnp.where(k_label > 0, k_label, -2)], axis=1).astype(F32)
    k_meta = jnp.pad(k_meta, ((0, 0), (0, 126)))
    heads = quarter // HEAD
    column = jnp.arange(heads, dtype=jnp.int32) * HEAD
    base = t * half + x * quarter
    column = jnp.where(column < own, base + c * own + column, base + (1 - c) * own + column - own)
    slopes = jnp.exp2(-((column // HEAD).astype(F32) + 1.0) * 0.5) * (4.0 / length)

    def columns(both, first, last):
        return both[0][:, first:last], both[1][:, first:last]

    def swap_halves(v):
        w = v.shape[-1] // 2
        return jnp.concatenate([v[:, w:], v[:, :w]], axis=-1)

    tokens_in = spread_input(hidden_in[0])
    grad_tokens = spread_input(out_grad[0])

    x_now = tokens_in[:rows].astype(F32)
    a = normalize(tokens_in.astype(F32), gain_one[0], shift_one[0]).astype(BF)
    kept = []
    for layer in range(layers):
        both = attention_both[layer]
        w_qkv = columns(both, 0, 3 * own)
        w_dense = columns(both, 3 * own, 4 * own)
        parts = [mm(a, w, NN) for w in w_qkv]
        pick = lambda n: jnp.concatenate([p[:, n * own : (n + 1) * own] for p in parts], axis=1)
        q = (pick(0) + bias_qv[layer, 0]).astype(BF)
        k_here = pick(1).astype(BF)
        v_here = (pick(2) + bias_qv[layer, 1]).astype(BF)
        other = fetch(jnp.concatenate([swap_halves(k_here), swap_halves(v_here)], axis=1), 0, 1, 0)
        k = jnp.concatenate([k_here, other[:, :quarter]], axis=0)
        v = jnp.concatenate([v_here, other[:, quarter:]], axis=0)
        o, lse = attend_forward(slopes, q_meta, k_meta, q, k, v)
        branch = mm(o[:, :own], w_dense[0], NT) + mm(o[:, own:], w_dense[1], NT)
        middle = x_now + (scatter(branch) + bias_dense[layer])
        a2 = gather(normalize(middle, gain_two[layer], shift_two[layer]).astype(BF))
        w_up = columns(feed_both[layer], 0, hidden_own)
        w_down = columns(feed_both[layer], hidden_own, 2 * hidden_own)
        u = [
            mm(a2, w_up[i], NN) + bias_up[layer, i * hidden_own : (i + 1) * hidden_own] for i in range(2)
        ]
        g = [gelu_tanh(v).astype(BF) for v in u]
        branch = mm(g[0], w_down[0], NT) + mm(g[1], w_down[1], NT)
        kept.append((x_now, a, q, k, v, o, lse, middle, a2, u, g))
        x_now = middle + (scatter(branch) + bias_down[layer])
        if layer + 1 < layers:
            a = gather(normalize(x_now, gain_one[layer + 1], shift_one[layer + 1]).astype(BF))

    def join_rows(v):
        parts = jnp.stack([v] + [fetch(v, 0, 0, dt) for dt in range(1, tp)])
        return jnp.concatenate(
            [lax.dynamic_index_in_dim(parts, (j - t) % tp, 0, keepdims=False) for j in range(tp)], axis=0
        )

    hidden_out = join_rows(x_now.astype(BF))

    def share_out(grad_own, grad_other):
        total = grad_own + fetch(grad_other.astype(BF), 0, 1, 0).astype(F32)
        return lax.psum_scatter(total.astype(BF), "fsdp", scatter_dimension=0, tiled=True)

    def spread_columns(v):
        outer_parts = jnp.stack([v] + [fetch(v, dx, 0, 0) for dx in range(1, outer)])
        parts = jnp.stack([outer_parts, fetch(outer_parts, 0, 1, 0)])
        return [
            lax.dynamic_index_in_dim(
                lax.dynamic_index_in_dim(parts, (cj - c) % 2, 0, keepdims=False), (xj - x) % outer, 0, keepdims=False
            )
            for xj in range(outer)
            for cj in range(2)
        ]

    def small_sums(rows_d, up_sum, qv_sum):
        up_full = jnp.zeros((hidden_half,), F32)
        up_full = lax.dynamic_update_slice_in_dim(up_full, up_sum[:hidden_own], (x * 2 + c) * hidden_own, 0)
        up_full = lax.dynamic_update_slice_in_dim(up_full, up_sum[hidden_own:], (x * 2 + 1 - c) * hidden_own, 0)
        qv_full = jnp.zeros((2, half), F32)
        qv_full = lax.dynamic_update_slice_in_dim(qv_full, qv_sum[:, :own], (x * 2 + c) * own, 1)
        qv_full = lax.dynamic_update_slice_in_dim(qv_full, qv_sum[:, own:], (x * 2 + 1 - c) * own, 1)
        per_f = jnp.concatenate(
            [
                jnp.stack(rows_d).reshape(6, fsdp, rows_f).transpose(1, 0, 2).reshape(fsdp, -1),
                up_full.reshape(blocks_up, fsdp, lane_f).transpose(1, 0, 2).reshape(fsdp, -1),
                qv_full.reshape(2 * blocks_qv, fsdp, lane_f).transpose(1, 0, 2).reshape(fsdp, -1),
            ],
            axis=1,
        )
        width = per_f.shape[1]
        per_f = jnp.pad(per_f, ((0, 0), (0, -width % 1024))).reshape(fsdp, -1, 128)
        per_f = per_f + fetch(per_f, 0, 1, 0)
        total = lax.dynamic_index_in_dim(per_f, f, 0, keepdims=False)
        for df in range(1, fsdp):
            piece = lax.dynamic_index_in_dim(per_f, (f + df) % fsdp, 0, keepdims=False)
            total = total + fetch_f(piece, -df)
        terms = total
        for dx in range(1, outer):
            total = total + fetch(terms, dx, 0, 0)
        terms = total
        across = total
        for dt in range(1, tp):
            across = across + fetch(terms, 0, 0, dt)
        flat, flat_across = total.reshape(-1), across.reshape(-1)
        first = 6 * rows_f
        last = first + blocks_up * lane_f
        return (
            flat_across[:first].reshape(6, rows_f),
            flat[first:last].reshape(blocks_up, lane_f),
            flat[last : last + 2 * blocks_qv * lane_f].reshape(2, blocks_qv, lane_f),
        )

    grad_x = grad_tokens[:rows].astype(F32)
    dy2 = grad_tokens
    done = [None] * layers
    for layer in reversed(range(layers)):
        x_old, a, q, k, v, o, lse, middle, a2, u, g = kept[layer]
        w_up = columns(feed_both[layer], 0, hidden_own)
        w_down = columns(feed_both[layer], hidden_own, 2 * hidden_own)
        both = attention_both[layer]
        w_qkv = columns(both, 0, 3 * own)
        w_dense = columns(both, 3 * own, 4 * own)

        sum_down = jnp.sum(dy2[:rows].astype(F32), axis=0)
        du = [(mm(dy2, w_down[i], NN) * gelu_slope(u[i])).astype(BF) for i in range(2)]
        da2 = scatter(mm(du[0], w_up[0], NT) + mm(du[1], w_up[1], NT))
        feed_terms = [jnp.concatenate([mm(a2, du[i], TN), mm(dy2, g[i], TN)], axis=1) for i in range(2)]
        feed_grad = share_out(*feed_terms)
        sum_up = jnp.concatenate([jnp.sum(v.astype(F32), axis=0) for v in du])

        grad_mid, sum_gain_two, sum_shift_two = normalize_back(middle, gain_two[layer], da2)
        grad_mid = grad_x + grad_mid
        dy1_own = grad_mid.astype(BF)
        sum_dense = jnp.sum(dy1_own.astype(F32), axis=0)
        dy1 = gather(dy1_own)
        do = jnp.concatenate([mm(dy1, w, NN).astype(BF) for w in w_dense], axis=1)
        dq, dk, dv = attend_backward(slopes, q_meta, k_meta, q, k, v, do, lse)
        tokens = dq.shape[0]
        other = fetch(
            jnp.concatenate([swap_halves(dk[tokens:]), swap_halves(dv[tokens:])], axis=1), 0, 1, 0
        ).astype(F32)
        dk = (dk[:tokens].astype(F32) + other[:, :quarter]).astype(BF)
        dv = (dv[:tokens].astype(F32) + other[:, quarter:]).astype(BF)
        dqkv = [jnp.concatenate([w[:, i * own : (i + 1) * own] for w in (dq, dk, dv)], axis=1) for i in range(2)]
        da = scatter(mm(dqkv[0], w_qkv[0], NT) + mm(dqkv[1], w_qkv[1], NT))
        attention_terms = [
            jnp.concatenate([mm(a, dqkv[i], TN), mm(dy1, o[:, i * own : (i + 1) * own], TN)], axis=1) for i in range(2)
        ]
        attention_grad = share_out(*attention_terms)
        sum_qv = jnp.stack([jnp.sum(dq.astype(F32), axis=0), jnp.sum(dv.astype(F32), axis=0)])
        grad_in, sum_gain_one, sum_shift_one = normalize_back(x_old, gain_one[layer], da)
        grad_x = grad_mid + grad_in
        if layer > 0:
            dy2 = gather(grad_x.astype(BF))
        smalls_out = small_sums(
            [sum_gain_one, sum_shift_one, sum_dense, sum_gain_two, sum_shift_two, sum_down], sum_up, sum_qv
        )
        attention_parts = spread_columns(attention_grad)
        feed_parts = spread_columns(feed_grad)
        done[layer] = (
            smalls_out[0],
            smalls_out[1],
            smalls_out[2],
            jnp.concatenate([p[:, : 3 * own].reshape(rows_f, 3, own) for p in attention_parts], axis=2).astype(F32),
            jnp.concatenate([p[:, 3 * own :].T for p in attention_parts], axis=0).astype(F32),
            jnp.concatenate([p[:, :hidden_own] for p in feed_parts], axis=1).astype(F32),
            jnp.concatenate([p[:, hidden_own:].T for p in feed_parts], axis=0).astype(F32),
        )

    input_grad = join_rows(grad_x)
    rows_out = jnp.stack([entry[0] for entry in done])
    return (
        hidden_out[None],
        input_grad[None],
        rows_out[:, 0],
        rows_out[:, 1],
        jnp.stack([entry[3] for entry in done]),
        jnp.stack([entry[2] for entry in done]),
        jnp.stack([entry[4] for entry in done]),
        rows_out[:, 2],
        rows_out[:, 3],
        rows_out[:, 4],
        jnp.stack([entry[5] for entry in done]),
        jnp.stack([entry[1] for entry in done]),
        jnp.stack([entry[6] for entry in done]),
        rows_out[:, 5],
    )


def solution(mesh):
    tokens = P("fsdp", "ctx", None)
    vector = P(None, "fsdp")
    weights = (
        vector,
        vector,
        P(None, "fsdp", None, "tp"),
        P(None, None, "tp", "fsdp"),
        P(None, "tp", "fsdp"),
        vector,
        vector,
        vector,
        P(None, "fsdp", "tp"),
        P(None, "tp", "fsdp"),
        P(None, "tp", "fsdp"),
        vector,
    )
    body = functools.partial(local, mesh.shape["fsdp"], mesh.shape["ctx"] // 2, mesh.shape["tp"])
    return jax.shard_map(
        body,
        mesh=mesh,
        in_specs=(tokens, P("fsdp", None)) + weights + (tokens,),
        out_specs=(tokens, tokens) + weights,
        check_vma=False,
    )
```

```python
import functools
import math

import jax
import jax.numpy as jnp
from jax import lax
from jax.experimental import pallas as pl
from jax.experimental.layout import Layout, with_layout_constraint
from jax.experimental.pallas import tpu as pltpu
from jax.sharding import PartitionSpec as P

HEAD = 64
PIECE = 256
FAR = 1e30
BF = jnp.bfloat16
F32 = jnp.float32
INV_ROOT = 1.0 / math.sqrt(HEAD)
NT = (((1,), (1,)), ((), ()))
TN = (((0,), (0,)), ((), ()))
NN = (((1,), (0,)), ((), ()))


def mm(a, b, dims):
    return lax.dot_general(a, b, dims, preferred_element_type=F32)


def row_major(v):
    return with_layout_constraint(v, Layout(major_to_minor=tuple(range(v.ndim))))


def together(*values):
    return lax.optimization_barrier(values)


def after(values, *others):
    flat, tree = jax.tree.flatten(values)
    anywhere = pl.BlockSpec(memory_space=pl.ANY)
    out = pl.pallas_call(
        lambda *refs: None,
        in_specs=[anywhere] * (len(flat) + len(others)),
        out_specs=[anywhere] * len(flat),
        out_shape=[jax.ShapeDtypeStruct(v.shape, v.dtype) for v in flat],
        input_output_aliases={i: i for i in range(len(flat))},
        cost_estimate=pl.CostEstimate(flops=0, bytes_accessed=0, transcendentals=0),
        name="after",
    )(*flat, *others)
    return jax.tree.unflatten(tree, out)


def reach(q_meta_ref, k_meta_ref):
    delta = q_meta_ref[0:1, :] - k_meta_ref[:, 0:1]
    seen = (delta >= 0.0) | (q_meta_ref[1:2, :] == k_meta_ref[:, 1:2])
    return jnp.where(seen, jnp.abs(delta), FAR)


def lanes_of(width, head):
    lane = lax.broadcasted_iota(jnp.int32, (1, width), 1)
    return (lane // HEAD) == head


def forward_kernel(slope_ref, q_meta_ref, k_meta_ref, q_ref, k_ref, v_ref, o_ref, lse_ref, *, width):
    dist = reach(q_meta_ref, k_meta_ref)
    pairs = q_ref.shape[1] // width
    per = width // HEAD
    for pair in range(pairs):
        at = slice(pair * width, (pair + 1) * width)
        q = q_ref[:, at] * jnp.asarray(INV_ROOT, BF)
        k = k_ref[:, at]
        v = v_ref[:, at]
        outs = []
        for head in range(per):
            index = pair * per + head
            q_head = q if per == 1 else jnp.where(lanes_of(width, head), q, jnp.zeros_like(q))
            s = mm(k, q_head, NT) - slope_ref[index] * dist
            top = jnp.max(s, axis=0, keepdims=True)
            e = jnp.exp(s - top)
            z = jnp.sum(e, axis=0, keepdims=True)
            lse_ref[index : index + 1, :] = top + jnp.log(z)
            outs.append(mm(v, e.astype(BF), TN) / z)
        if per == 1:
            out = outs[0]
        else:
            row = lax.broadcasted_iota(jnp.int32, (width, 1), 0)
            out = jnp.where(row < HEAD, outs[0], outs[1])
        o_ref[:, at] = out.T.astype(BF)


def backward_kernel(
    slope_ref, q_meta_ref, k_meta_ref, q_ref, k_ref, v_ref, do_ref, lse_ref, dq_ref, dk_ref, dv_ref, dk_acc, dv_acc, *, width
):
    step = pl.program_id(0)

    @pl.when(step == 0)
    def _():
        dk_acc[...] = jnp.zeros_like(dk_acc)
        dv_acc[...] = jnp.zeros_like(dv_acc)

    dist = reach(q_meta_ref, k_meta_ref)
    pairs = q_ref.shape[1] // width
    per = width // HEAD
    for pair in range(pairs):
        at = slice(pair * width, (pair + 1) * width)
        q = q_ref[:, at] * jnp.asarray(INV_ROOT, BF)
        k = k_ref[:, at]
        v = v_ref[:, at]
        do = do_ref[:, at]
        dqs = []
        for head in range(per):
            index = pair * per + head
            mine = None if per == 1 else lanes_of(width, head)
            q_head = q if per == 1 else jnp.where(mine, q, jnp.zeros_like(q))
            do_head = do if per == 1 else jnp.where(mine, do, jnp.zeros_like(do))
            s = mm(k, q_head, NT) - slope_ref[index] * dist
            p = jnp.exp(s - lse_ref[index : index + 1, :])
            dp = mm(v, do_head, NT)
            inner = jnp.sum(p * dp, axis=0, keepdims=True)
            ds = (p * (dp - inner)).astype(BF)
            dqs.append(mm(k, ds, TN))
            dk_acc[:, at] += mm(ds, q_head, NN)
            dv_acc[:, at] += mm(p.astype(BF), do_head, NN)
        if per == 1:
            dq = dqs[0]
        else:
            row = lax.broadcasted_iota(jnp.int32, (width, 1), 0)
            dq = jnp.where(row < HEAD, dqs[0], dqs[1])
        dq_ref[:, at] = (dq.T * INV_ROOT).astype(BF)

    @pl.when(step == pl.num_programs(0) - 1)
    def _():
        dk_ref[...] = dk_acc[...].astype(BF)
        dv_ref[...] = dv_acc[...].astype(BF)


def attention_setup(q, k):
    tokens, columns = q.shape
    keys = k.shape[0]
    width = min(128, columns)
    block = min(tokens, 256 if keys <= 1024 else 128)
    heads = columns // HEAD
    whole = lambda shape: pl.BlockSpec(shape, lambda i: (0,) * len(shape))
    specs = [
        pl.BlockSpec(memory_space=pltpu.SMEM),
        pl.BlockSpec((8, block), lambda i: (0, i)),
        whole((keys, 128)),
        pl.BlockSpec((block, columns), lambda i: (i, 0)),
        whole((keys, columns)),
        whole((keys, columns)),
    ]
    return tokens, columns, keys, width, block, heads, whole, specs


def attend_forward(slopes, q_meta, k_meta, q, k, v):
    tokens, columns, keys, width, block, heads, whole, specs = attention_setup(q, k)
    return pl.pallas_call(
        functools.partial(forward_kernel, width=width),
        grid=(tokens // block,),
        in_specs=specs,
        out_specs=[
            pl.BlockSpec((block, columns), lambda i: (i, 0)),
            pl.BlockSpec((heads, block), lambda i: (0, i)),
        ],
        out_shape=[
            jax.ShapeDtypeStruct((tokens, columns), BF),
            jax.ShapeDtypeStruct((heads, tokens), F32),
        ],
        compiler_params=pltpu.CompilerParams(vmem_limit_bytes=40 * 2**20),
        cost_estimate=pl.CostEstimate(
            flops=0, bytes_accessed=4 * keys * columns * 2, transcendentals=0
        ),
        name="attend_forward",
    )(slopes, q_meta, k_meta, q, k, v)


def attend_backward(slopes, q_meta, k_meta, q, k, v, do, lse):
    tokens, columns, keys, width, block, heads, whole, specs = attention_setup(q, k)
    return pl.pallas_call(
        functools.partial(backward_kernel, width=width),
        grid=(tokens // block,),
        in_specs=specs
        + [
            pl.BlockSpec((block, columns), lambda i: (i, 0)),
            pl.BlockSpec((heads, block), lambda i: (0, i)),
        ],
        out_specs=[
            pl.BlockSpec((block, columns), lambda i: (i, 0)),
            whole((keys, columns)),
            whole((keys, columns)),
        ],
        out_shape=[
            jax.ShapeDtypeStruct((tokens, columns), BF),
            jax.ShapeDtypeStruct((keys, columns), BF),
            jax.ShapeDtypeStruct((keys, columns), BF),
        ],
        scratch_shapes=[pltpu.VMEM((keys, columns), F32), pltpu.VMEM((keys, columns), F32)],
        compiler_params=pltpu.CompilerParams(vmem_limit_bytes=40 * 2**20),
        cost_estimate=pl.CostEstimate(
            flops=0, bytes_accessed=8 * keys * columns * 2, transcendentals=0
        ),
        name="attend_backward",
    )(slopes, q_meta, k_meta, q, k, v, do, lse)


def place_kernel(layer, split, order_ref, *refs):
    parts, (flat_ref, turned_ref) = refs[: order_ref.shape[0]], refs[-2:]
    step = pl.program_id(0)
    for i, part_ref in enumerate(parts):

        @pl.when(step == i)
        def _():
            wide = turned_ref.shape[1]
            if split == 1:
                flat_ref[0] = part_ref[:, :wide].astype(F32)
            else:
                for n in range(split):
                    flat_ref[0, n] = part_ref[:, n * wide : (n + 1) * wide].astype(F32)
            turned_ref[0] = part_ref[:, split * wide :].astype(F32).T


def place_plainly(layer, layers, split, order, parts, outs):
    wide = parts[0].shape[1] // (split + 1)
    if not outs:
        rows_f, blocks = parts[0].shape[0], len(parts)
        flat = (layers, rows_f, wide * blocks) if split == 1 else (layers, split, rows_f, wide * blocks)
        outs = jnp.zeros(flat, F32), jnp.zeros((layers, wide * blocks, rows_f), F32)
    flat, turned = outs
    for i, part in enumerate(parts):
        v = part.astype(F32)
        if split == 1:
            flat = lax.dynamic_update_slice(flat, v[None, :, :wide], (layer, 0, order[i] * wide))
        else:
            for n in range(split):
                flat = lax.dynamic_update_slice(
                    flat, v[None, None, :, n * wide : (n + 1) * wide], (layer, n, 0, order[i] * wide)
                )
        turned = lax.dynamic_update_slice(turned, v[:, split * wide :].T[None], (layer, order[i] * wide, 0))
    return flat, turned


def place(layer, layers, split, order, parts, outs):
    rows_f, wide = parts[0].shape[0], parts[0].shape[1] // (split + 1)
    blocks = len(parts)
    if wide % 128:
        return place_plainly(layer, layers, split, order, parts, outs)
    if split == 1:
        flat = jax.ShapeDtypeStruct((layers, rows_f, wide * blocks), F32)
        flat_spec = pl.BlockSpec((1, rows_f, wide), lambda i, order: (layer, 0, order[i]))
    else:
        flat = jax.ShapeDtypeStruct((layers, split, rows_f, wide * blocks), F32)
        flat_spec = pl.BlockSpec((1, split, rows_f, wide), lambda i, order: (layer, 0, 0, order[i]))
    return pl.pallas_call(
        functools.partial(place_kernel, layer, split),
        grid_spec=pltpu.PrefetchScalarGridSpec(
            num_scalar_prefetch=1,
            grid=(blocks,),
            in_specs=[pl.BlockSpec(part.shape, lambda i, order: (0, 0)) for part in parts]
            + [pl.BlockSpec(memory_space=pl.ANY) for _ in outs],
            out_specs=[flat_spec, pl.BlockSpec((1, wide, rows_f), lambda i, order: (layer, order[i], 0))],
        ),
        out_shape=[flat, jax.ShapeDtypeStruct((layers, wide * blocks, rows_f), F32)],
        input_output_aliases={1 + blocks + i: i for i in range(len(outs))},
        cost_estimate=pl.CostEstimate(flops=0, bytes_accessed=6 * rows_f * wide * (split + 1) * blocks, transcendentals=0),
        name="place",
    )(order, *parts, *outs)


def statistics(v):
    mean = jnp.mean(v, axis=-1, keepdims=True)
    centred = v - mean
    variance = jnp.mean(centred * centred, axis=-1, keepdims=True)
    scale = lax.rsqrt(variance + 1e-05)
    return centred * scale, scale


def normalize(v, gain, shift):
    return statistics(v)[0] * gain + shift


def normalize_back(v, gain, grad):
    hat, scale = statistics(v)
    pulled = grad * gain
    first = jnp.mean(pulled, axis=-1, keepdims=True)
    second = jnp.mean(pulled * hat, axis=-1, keepdims=True)
    return scale * (pulled - first - hat * second), jnp.sum(grad * hat, axis=0), jnp.sum(grad, axis=0)


C0 = math.sqrt(2.0 / math.pi)
C1 = 0.044715


def gelu_tanh(t):
    return 0.5 * t * (1.0 + jnp.tanh(C0 * (t + C1 * t * t * t)))


def gelu_slope(t):
    bent = jnp.tanh(C0 * (t + C1 * t * t * t))
    return 0.5 * (1.0 + bent) + 0.5 * t * (1.0 - bent * bent) * (C0 * (1.0 + 3.0 * C1 * t * t))


def local(
    fsdp,
    outer,
    tp,
    hidden_in,
    piece_starts,
    ln1_gain,
    ln1_shift,
    qkv_weight,
    qv_bias,
    dense_weight,
    dense_bias,
    ln2_gain,
    ln2_shift,
    up_weight,
    up_bias,
    down_weight,
    down_bias,
    out_grad,
):
    layers, rows_f, _, half = qkv_weight.shape
    group_len, d = hidden_in.shape[1:]
    hidden_half = up_weight.shape[2]
    quarter = half // outer
    own = quarter // 2
    hidden_quarter = hidden_half // outer
    hidden_own = hidden_quarter // 2
    rows = group_len // tp
    length = group_len * 2 * outer

    f = lax.axis_index("fsdp")
    ctx = lax.axis_index("ctx")
    t = lax.axis_index("tp")
    x, c = ctx // 2, ctx % 2

    def fetch(v, dx, dc, dt):
        pairs = []
        for xi in range(outer):
            for ci in range(2):
                for ti in range(tp):
                    src = (((xi + dx) % outer) * 2 + (ci + dc) % 2) * tp + (ti + dt) % tp
                    pairs.append((src, (xi * 2 + ci) * tp + ti))
        return lax.ppermute(v, ("ctx", "tp"), pairs)

    def fetch_f(v, df):
        return lax.ppermute(v, "fsdp", [((i + df) % fsdp, i) for i in range(fsdp)])

    slots = [(dx, dt) for dx in range(outer) for dt in range(tp)]

    def gather(v, also=None):
        parts = [fetch(v, dx, 0, dt) for dx, dt in slots[1:]]
        if also is not None:
            parts, also = together(parts, also)
        rows_all = jnp.concatenate([v, *parts], axis=0)
        return rows_all if also is None else (rows_all, also)

    def scatter(term, ahead=None):
        sent = term(rows, rows * len(slots)).astype(BF)
        came = [
            fetch(sent[(i - 1) * rows : i * rows], -dx, 0, -dt) for i, (dx, dt) in list(enumerate(slots))[:0:-1]
        ]
        total = term(0, rows)
        kept = None
        if ahead is not None:
            kept = ahead(sent)
            came, total, kept = together(came, total, kept)
        for part in came:
            total = total + part.astype(F32)
        return total if ahead is None else (total, kept)

    def spread_input(v):
        out = []
        for dx in range(outer):
            block = v if dx == 0 else fetch(v, dx, 0, 0)
            for dt in range(tp):
                out.append(lax.dynamic_slice_in_dim(block, ((t + dt) % tp) * rows, rows, 0))
        return jnp.concatenate(out, axis=0)

    at = (x * 2 + c) * own
    at_hidden = (x * 2 + c) * hidden_own

    def packs_of(layer):
        qkv = lax.dynamic_slice(qkv_weight, (layer, 0, 0, at), (1, rows_f, 3, own))[0].reshape(rows_f, 3 * own)
        dense = lax.dynamic_slice(dense_weight, (layer, at, 0), (1, own, rows_f))[0].T
        attention = row_major(jnp.concatenate([qkv, dense], axis=1))
        up = lax.dynamic_slice(up_weight, (layer, 0, at_hidden), (1, rows_f, hidden_own))[0]
        down = lax.dynamic_slice(down_weight, (layer, at_hidden, 0), (1, hidden_own, rows_f))[0].T
        return attention, row_major(jnp.concatenate([up, down], axis=1))

    packs = [pack for layer in range(layers) for pack in packs_of(layer)]
    packs[0], hidden_in, out_grad, ln1_gain, ln1_shift, dense_bias, ln2_gain, ln2_shift, down_bias, qv_bias, up_bias = together(
        packs[0], hidden_in, out_grad, ln1_gain, ln1_shift, dense_bias, ln2_gain, ln2_shift, down_bias, qv_bias, up_bias
    )
    first = lax.all_gather(packs[0], "fsdp", axis=0, tiled=True)
    first, *rest = together(first, *packs[1:])
    full = [first] + [lax.all_gather(w, "fsdp", axis=0, tiled=True) for w in rest]
    attention_own, feed_own = full[0::2], full[1::2]

    def with_other(own, *others):
        if others:
            own = after(own, *others)
        return own, fetch(own, 0, 1, 0)

    attention_both, feed_both = [with_other(attention_own[0])], []

    blocks_qv, lane_f = qv_bias.shape[2:]
    blocks_up = up_bias.shape[1]
    narrow = jnp.concatenate([qv_bias.reshape(-1, lane_f), up_bias.reshape(-1, lane_f)], axis=0)
    narrow = jnp.pad(narrow, ((0, -(6 * layers + narrow.shape[0]) % 16), (0, rows_f - lane_f)))
    small = jnp.concatenate([ln1_gain, ln1_shift, dense_bias, ln2_gain, ln2_shift, down_bias, narrow], axis=0)
    held = jnp.stack([small] + [fetch_f(small, k) for k in range(1, fsdp)])
    held = [lax.dynamic_index_in_dim(held, (j - f) % fsdp, 0, keepdims=False) for j in range(fsdp)]
    vectors = jnp.concatenate([v[: 6 * layers] for v in held], axis=1).astype(F32)
    gain_one, shift_one, bias_dense, gain_two, shift_two, bias_down = (
        vectors[n * layers : (n + 1) * layers] for n in range(6)
    )
    spot = 6 * layers
    narrow = jnp.concatenate([v[spot:, :lane_f] for v in held], axis=1).astype(F32)
    bias_qv = narrow[: layers * 2 * blocks_qv].reshape(layers, 2, half)
    bias_up = narrow[layers * 2 * blocks_qv : layers * (2 * blocks_qv + blocks_up)].reshape(layers, hidden_half)

    def own_first(v, width):
        mine = lax.dynamic_slice_in_dim(v, (x * 2 + c) * width, width, v.ndim - 1)
        others = lax.dynamic_slice_in_dim(v, (x * 2 + 1 - c) * width, width, v.ndim - 1)
        return jnp.concatenate([mine, others], axis=-1)

    bias_qv = own_first(bias_qv, own)
    bias_up = own_first(bias_up, hidden_own)

    row_ids = jnp.arange(rows, dtype=jnp.int32)

    def positions_of(core):
        return jnp.concatenate(
            [
                (((x + dx) % outer) * 2 + core) * group_len + ((t + dt) % tp) * rows + row_ids
                for dx, dt in slots
            ]
        )

    def labels_of(positions):
        starts = piece_starts[0]
        inside = (positions[None, :] >= starts[:, None]) & (positions[None, :] < starts[:, None] + PIECE)
        ids = jnp.arange(1, starts.shape[0] + 1, dtype=jnp.int32)
        return jnp.sum(jnp.where(inside, ids[:, None], 0), axis=0)

    here, there = positions_of(c), positions_of(1 - c)
    keys_at = jnp.concatenate([here, there])
    q_label = labels_of(here)
    k_label = labels_of(keys_at)
    q_meta = jnp.stack([here, jnp.where(q_label > 0, q_label, -1)]).astype(F32)
    q_meta = jnp.pad(q_meta, ((0, 6), (0, 0)))
    k_meta = jnp.stack([keys_at, jnp.where(k_label > 0, k_label, -2)], axis=1).astype(F32)
    k_meta = jnp.pad(k_meta, ((0, 0), (0, 126)))
    heads = quarter // HEAD
    column = jnp.arange(heads, dtype=jnp.int32) * HEAD
    base = t * half + x * quarter
    column = jnp.where(column < own, base + c * own + column, base + (1 - c) * own + column - own)
    slopes = jnp.exp2(-((column // HEAD).astype(F32) + 1.0) * 0.5) * (4.0 / length)

    def columns(both, first, last):
        return both[0][:, first:last], both[1][:, first:last]

    def swap_halves(v):
        w = v.shape[-1] // 2
        return jnp.concatenate([v[:, w:], v[:, :w]], axis=-1)

    tokens_in = spread_input(hidden_in[0])
    grad_tokens = spread_input(out_grad[0])

    def feed_terms_of(layer, g):
        w_down = columns(feed_both[layer], hidden_own, 2 * hidden_own)
        return lambda i, j: mm(g[0][i:j], w_down[0], NT) + mm(g[1][i:j], w_down[1], NT)

    def feed_sum(layer, term):
        return kept[layer][7] + (scatter(term) + bias_down[layer])

    x_now = tokens_in[:rows].astype(F32)
    a = normalize(tokens_in.astype(F32), gain_one[0], shift_one[0]).astype(BF)
    kept = []
    for layer in range(layers):
        both = attention_both[layer]
        w_qkv = columns(both, 0, 3 * own)
        w_dense = columns(both, 3 * own, 4 * own)
        parts = [mm(a, w, NN) for w in w_qkv]
        pick = lambda n: jnp.concatenate([p[:, n * own : (n + 1) * own] for p in parts], axis=1)
        q = (pick(0) + bias_qv[layer, 0]).astype(BF)
        k_here = pick(1).astype(BF)
        v_here = (pick(2) + bias_qv[layer, 1]).astype(BF)
        other = fetch(jnp.concatenate([swap_halves(k_here), swap_halves(v_here)], axis=1), 0, 1, 0)
        k = jnp.concatenate([k_here, other[:, :quarter]], axis=0)
        v = jnp.concatenate([v_here, other[:, quarter:]], axis=0)
        o, lse = attend_forward(slopes, q_meta, k_meta, q, k, v)
        branch = lambda i, j: mm(o[i:j, :own], w_dense[0], NT) + mm(o[i:j, own:], w_dense[1], NT)
        middle = x_now + (scatter(branch) + bias_dense[layer])
        a2 = gather(normalize(middle, gain_two[layer], shift_two[layer]).astype(BF))
        feed_both.append(with_other(feed_own[layer], middle if layer else a2))
        w_up = columns(feed_both[layer], 0, hidden_own)
        u = [
            mm(a2, w_up[i], NN) + bias_up[layer, i * hidden_own : (i + 1) * hidden_own] for i in range(2)
        ]
        g = [gelu_tanh(v).astype(BF) for v in u]
        kept.append((x_now, a, q, k, v, o, lse, middle, a2, u, g))
        if layer + 1 < layers:
            x_now = feed_sum(layer, feed_terms_of(layer, g))
            a = gather(normalize(x_now, gain_one[layer + 1], shift_one[layer + 1]).astype(BF))
            attention_both.append(with_other(attention_own[layer + 1], x_now))

    def join_rows(v):
        parts = jnp.stack([v] + [fetch(v, 0, 0, dt) for dt in range(1, tp)])
        return jnp.concatenate(
            [lax.dynamic_index_in_dim(parts, (j - t) % tp, 0, keepdims=False) for j in range(tp)], axis=0
        )

    def share_cores(pairs):
        sent = jnp.concatenate([mm(v, other, TN).astype(BF) for v, _, other in pairs], axis=1)
        came = fetch(row_major(sent), 0, 1, 0)
        total, spot = [], 0
        for v, mine, _ in pairs:
            wide = mine.shape[1]
            total.append((mm(v, mine, TN) + came[:, spot : spot + wide].astype(F32)).astype(BF))
            spot += wide
        return row_major(jnp.concatenate(total, axis=1))

    def share_sequences(total):
        return lax.psum_scatter(total, "fsdp", scatter_dimension=0, tiled=True)

    order = jnp.stack([((x + dx) % outer) * 2 + (c + dc) % 2 for dc in range(2) for dx in range(outer)])

    def spread(v):
        return [v] + [fetch(v, dx, 0, 0) for dx in range(1, outer)]

    def both_cores(parts):
        return parts + [fetch(part, 0, 1, 0) for part in parts]

    def small_sums(rows_d, up_sum, qv_sum):
        up_full = jnp.zeros((layers, hidden_half), F32)
        up_full = lax.dynamic_update_slice_in_dim(up_full, up_sum[:, :hidden_own], (x * 2 + c) * hidden_own, 1)
        up_full = lax.dynamic_update_slice_in_dim(up_full, up_sum[:, hidden_own:], (x * 2 + 1 - c) * hidden_own, 1)
        qv_full = jnp.zeros((layers, 2, half), F32)
        qv_full = lax.dynamic_update_slice_in_dim(qv_full, qv_sum[:, :, :own], (x * 2 + c) * own, 2)
        qv_full = lax.dynamic_update_slice_in_dim(qv_full, qv_sum[:, :, own:], (x * 2 + 1 - c) * own, 2)
        per_f = jnp.concatenate(
            [
                rows_d.reshape(-1, fsdp, rows_f).transpose(1, 0, 2).reshape(fsdp, -1),
                up_full.reshape(-1, fsdp, lane_f).transpose(1, 0, 2).reshape(fsdp, -1),
                qv_full.reshape(-1, fsdp, lane_f).transpose(1, 0, 2).reshape(fsdp, -1),
            ],
            axis=1,
        )
        width = per_f.shape[1]
        per_f = jnp.pad(per_f, ((0, 0), (0, -width % 1024))).reshape(fsdp, -1, 128)
        per_f = per_f + fetch(per_f, 0, 1, 0)
        total = lax.dynamic_index_in_dim(per_f, f, 0, keepdims=False)
        for df in range(1, fsdp):
            piece = lax.dynamic_index_in_dim(per_f, (f + df) % fsdp, 0, keepdims=False)
            total = total + fetch_f(piece, -df)
        terms = total
        for dx in range(1, outer):
            total = total + fetch(terms, dx, 0, 0)
        terms = total
        across = total
        for dt in range(1, tp):
            across = across + fetch(terms, 0, 0, dt)
        flat, flat_across = total.reshape(-1), across.reshape(-1)
        first = layers * 6 * rows_f
        last = first + layers * blocks_up * lane_f
        return (
            flat_across[:first].reshape(layers, 6, rows_f),
            flat[first:last].reshape(layers, blocks_up, lane_f),
            flat[last : last + layers * 2 * blocks_qv * lane_f].reshape(layers, 2, blocks_qv, lane_f),
        )

    grad_x = grad_tokens[:rows].astype(F32)
    dy2 = grad_tokens
    small_terms = [None] * layers
    held_feed = held_attention = None
    for layer in reversed(range(layers)):
        x_old, a, q, k, v, o, lse, middle, a2, u, g = kept[layer]
        w_up = columns(feed_both[layer], 0, hidden_own)
        w_down = columns(feed_both[layer], hidden_own, 2 * hidden_own)
        both = attention_both[layer]
        w_qkv = columns(both, 0, 3 * own)
        w_dense = columns(both, 3 * own, 4 * own)

        sum_down = jnp.sum(dy2[:rows].astype(F32), axis=0)
        du = [(mm(dy2, w_down[i], NN) * gelu_slope(u[i])).astype(BF) for i in range(2)]
        if layer + 1 < layers:
            *du, held_attention = together(*du, held_attention)
        da2, feed_terms = scatter(
            lambda i, j: mm(du[0][i:j], w_up[0], NT) + mm(du[1][i:j], w_up[1], NT),
            lambda _: share_cores([(a2, du[0], du[1]), (dy2, g[0], g[1])]),
        )
        feed_grad = share_sequences(feed_terms)
        sum_up = jnp.concatenate([jnp.sum(v.astype(F32), axis=0) for v in du])

        grad_mid, sum_gain_two, sum_shift_two = normalize_back(middle, gain_two[layer], da2)
        grad_mid = grad_x + grad_mid
        dy1_own = grad_mid.astype(BF)
        sum_dense = jnp.sum(dy1_own.astype(F32), axis=0)
        if layer + 1 == layers:
            term = feed_terms_of(layer, g)
            dy1 = gather(dy1_own)
            last_terms, _ = together([term(0, rows), term(rows, rows * len(slots)).astype(BF)], dy1)
            last_sum = feed_sum(layer, lambda i, j: last_terms[min(i, 1)])
        else:
            dy1 = gather(dy1_own)
            held_attention, held_feed, _ = together(held_attention, held_feed, dy1)
            earlier = both_cores(spread(held_attention)), both_cores(spread(held_feed))
        do = jnp.concatenate([mm(dy1, w, NN).astype(BF) for w in w_dense], axis=1)
        dq, dk, dv = attend_backward(slopes, q_meta, k_meta, q, k, v, do, lse)
        tokens = dq.shape[0]
        other = fetch(
            jnp.concatenate([swap_halves(dk[tokens:]), swap_halves(dv[tokens:])], axis=1), 0, 1, 0
        )
        other, feed_grad = together(other, feed_grad)
        other = other.astype(F32)
        dk = (dk[:tokens].astype(F32) + other[:, :quarter]).astype(BF)
        dv = (dv[:tokens].astype(F32) + other[:, quarter:]).astype(BF)
        dqkv = [jnp.concatenate([w[:, i * own : (i + 1) * own] for w in (dq, dk, dv)], axis=1) for i in range(2)]

        def meanwhile(sent):
            terms = share_cores([(a, dqkv[0], dqkv[1]), (dy1, o[:, :own], o[:, own:])])
            if layer + 1 == layers:
                return terms, (), ()
            return terms, place(1, layers, 3, order, earlier[0], ()), place(1, layers, 1, order, earlier[1], ())

        da, (attention_terms, attention_outs, feed_outs) = scatter(
            lambda i, j: mm(dqkv[0][i:j], w_qkv[0], NT) + mm(dqkv[1][i:j], w_qkv[1], NT), meanwhile
        )
        held_attention = share_sequences(attention_terms)
        sum_qv = jnp.stack([jnp.sum(dq.astype(F32), axis=0), jnp.sum(dv.astype(F32), axis=0)])
        grad_in, sum_gain_one, sum_shift_one = normalize_back(x_old, gain_one[layer], da)
        grad_x = grad_mid + grad_in
        held_feed = feed_grad
        if layer > 0:
            dy2 = gather(grad_x.astype(BF))
        small_terms[layer] = (
            jnp.stack([sum_gain_one, sum_shift_one, sum_dense, sum_gain_two, sum_shift_two, sum_down]),
            sum_up,
            sum_qv,
        )

    hidden_out = join_rows(together(last_sum.astype(BF), attention_terms)[0])
    up_grad, down_grad = place(0, layers, 1, order, both_cores(spread(held_feed)), feed_outs)
    qkv_grad, dense_grad = place(0, layers, 3, order, both_cores(spread(held_attention)), attention_outs)
    rows_out, up_out, qv_out = small_sums(*(jnp.stack(v) for v in zip(*small_terms)))
    input_grad = join_rows(grad_x)
    return (
        hidden_out[None],
        input_grad[None],
        rows_out[:, 0],
        rows_out[:, 1],
        jnp.transpose(qkv_grad, (0, 2, 1, 3)),
        qv_out,
        dense_grad,
        rows_out[:, 2],
        rows_out[:, 3],
        rows_out[:, 4],
        up_grad,
        up_out,
        down_grad,
        rows_out[:, 5],
    )


def solution(mesh):
    tokens = P("fsdp", "ctx", None)
    vector = P(None, "fsdp")
    weights = (
        vector,
        vector,
        P(None, "fsdp", None, "tp"),
        P(None, None, "tp", "fsdp"),
        P(None, "tp", "fsdp"),
        vector,
        vector,
        vector,
        P(None, "fsdp", "tp"),
        P(None, "tp", "fsdp"),
        P(None, "tp", "fsdp"),
        vector,
    )
    body = functools.partial(local, mesh.shape["fsdp"], mesh.shape["ctx"] // 2, mesh.shape["tp"])
    return jax.shard_map(
        body,
        mesh=mesh,
        in_specs=(tokens, P("fsdp", None)) + weights + (tokens,),
        out_specs=(tokens, tokens) + weights,
        check_vma=False,
    )
```
